32 devices in a mesh: seq: 16 (over z, x, core), head: 2 (over y).
Axes of the slice: x: 2, y: 2, z: 4, core: 2. Of those that a mesh axis runs over, the one named last changes fastest.
Arguments:
- queries: bfloat16 [4096, 1792], P('seq', 'head'), may hold values from -120 to 120
- key_rows: bfloat16 [4096, 256], P('seq', 'head'), may hold values from -9 to 9
- value_rows: bfloat16 [4096, 256], P('seq', 'head'), may hold values from -6 to 6
- out_weight: bfloat16 [1792, 3584], P('head', 'seq'), may hold values from -0.125 to 0.125
Outputs:
- projected: bfloat16 [4096, 3584], P('seq', 'head')
The draws below stay inside these ranges and needn't reach their ends.
All inputs are finite; a program needn't handle non-finite values.
Results may differ from the reference program's by a relative error of at most 0.009.
Values may be sent and summed in bfloat16 or wider, within the bound.
No kernel may reach another device: no remote copies, remote signals or barrier semaphores. Data moves between devices by JAX's collectives and lax.ppermute only.
A program may use at most 64 MiB of HBM per device.

```python
import math
import jax
import jax.numpy as jnp
from jax import lax

D = 3584
KVH = 2
QPK = 7
HD = 128
BLK = 256
TOKENS = 4096


def base_keys(key):
    normal_draw = jax.random.normal(jax.random.fold_in(key, 7101), (TOKENS, KVH * HD), jnp.float32)
    return jnp.clip(1.5 * normal_draw, -9.0, 9.0)


def draw_key_rows(key, part):
    keys_drawn = base_keys(key)
    return keys_drawn.astype(jnp.bfloat16)


def draw_queries(key, part):
    normal_draw = jax.random.normal(jax.random.fold_in(key, 7202), (TOKENS, KVH, QPK, HD), jnp.float32)
    drawn = jnp.clip(1.5 * normal_draw, -9.0, 9.0)
    return drawn.reshape(TOKENS, KVH * QPK * HD).astype(jnp.bfloat16)


def level_of(own_key, shape, cuts, low, largest):
    def one(axis_at, shards_of):
        heights = jax.random.uniform(jax.random.fold_in(jax.random.fold_in(own_key, 6), axis_at), (shards_of,), jnp.float32, low / len(cuts), largest / len(cuts))
        return jnp.repeat(jnp.exp(heights), shape[axis_at] // shards_of).reshape((-1,) + (1,) * (len(shape) - axis_at - 1))

    loudness = one(*cuts[0])
    for cut in cuts[1:]:
        loudness = loudness * one(*cut)
    return loudness


def bell_draw(own_key, shape, deviation, reach, cuts=(), kind=jnp.bfloat16):
    values = deviation * jax.random.normal(own_key, shape, jnp.float32)
    if cuts:
        values = values * level_of(own_key, shape, cuts, -0.22, 0.18)
    return jnp.clip(values, -reach, reach).astype(kind)


def setup_inputs(seed: int = 0) -> dict:
    keys = jax.random.split(jax.random.key(seed), 5)
    queries = draw_queries(jax.random.fold_in(keys[4], 71), 0)
    key_rows = draw_key_rows(jax.random.fold_in(keys[4], 71), 0)
    value_rows = bell_draw(keys[2], (TOKENS, KVH * HD), 1.0, 6.0, ((0, 16), (1, 2)))
    out_weight = bell_draw(keys[3], (KVH * QPK * HD, D), (KVH * QPK * HD) ** -0.5, 0.125, ((0, 2), (1, 16)))
    return {"queries": queries, "key_rows": key_rows, "value_rows": value_rows, "out_weight": out_weight}


def reference(queries, key_rows, value_rows, out_weight):
    block_count = TOKENS // BLK
    levels = block_count.bit_length() - 1
    score_scale = 1.0 / math.sqrt(HD)
    query_all = queries.reshape(block_count, BLK, KVH, QPK, HD)
    key_all = key_rows.reshape(block_count, BLK, KVH, HD)
    value_all = value_rows.reshape(block_count, BLK, KVH, HD)
    flip_masks = jnp.array([1 << level for level in range(1, levels)], dtype=jnp.int32)

    def one_block(block_number):
        beside_all = jnp.stack([block_number - 1, block_number, block_number + 1]).astype(jnp.int32)
        chosen = jnp.concatenate([beside_all, jnp.bitwise_xor(block_number, flip_masks).astype(jnp.int32)])
        usable = jnp.concatenate([jnp.stack([block_number > 0, block_number >= 0, block_number < block_count - 1]), jnp.ones(flip_masks.shape, dtype=bool)])
        clipped = jnp.clip(chosen, 0, block_count - 1).astype(jnp.int32)
        key_sel = key_all[clipped].reshape(-1, KVH, HD).astype(jnp.float32)
        value_sel = value_all[clipped].reshape(-1, KVH, HD).astype(jnp.float32)
        key_usable = jnp.repeat(usable, BLK)
        query_sel = query_all[block_number].astype(jnp.float32)
        scores = jnp.einsum('thqd,shd->hqts', query_sel, key_sel) * score_scale
        scores = jnp.where(key_usable, scores, -1e+30)
        peak = lax.optimization_barrier(jnp.max(scores, axis=-1, keepdims=True))
        weights = jnp.exp(scores - peak)
        weight_sum = lax.optimization_barrier(jnp.sum(weights, axis=-1))
        rounded = lax.optimization_barrier(weights.astype(jnp.bfloat16)).astype(jnp.float32)
        numerator = jnp.einsum('hqts,shd->thqd', rounded, value_sel)
        blended = numerator / jnp.transpose(weight_sum, (2, 0, 1))[..., None]
        attended = blended.astype(jnp.bfloat16).reshape(BLK, KVH * QPK * HD)
        return jnp.dot(attended, out_weight, preferred_element_type=jnp.float32).astype(jnp.bfloat16)
    result = lax.map(one_block, jnp.arange(block_count, dtype=jnp.int32))
    return result.reshape(TOKENS, D)
```

```python
import functools
import math

import jax
import jax.numpy as jnp
from jax import lax
from jax.experimental import pallas as pl
from jax.experimental.pallas import tpu as pltpu
from jax.sharding import PartitionSpec as P

HD = 128
BLK = 256

masked_score = -1e30
vmem_limit = 20 * 2**20
in_vmem = pl.BlockSpec(memory_space=pltpu.VMEM)


def call_kernel(body, out_shape, operands, scratch=(), flops=0, moved=0, transcendentals=0):
    many = isinstance(out_shape, (list, tuple))
    return pl.pallas_call(
        body,
        out_shape=out_shape,
        in_specs=[in_vmem] * len(operands),
        out_specs=[in_vmem] * len(out_shape) if many else in_vmem,
        scratch_shapes=list(scratch),
        compiler_params=pltpu.CompilerParams(vmem_limit_bytes=vmem_limit),
        cost_estimate=pl.CostEstimate(
            flops=flops, bytes_accessed=moved, transcendentals=transcendentals
        ),
    )(*operands)


def flip(value, mask):
    pairs = [(source, source ^ mask) for source in range(lax.axis_size("seq"))]
    return lax.ppermute(value, "seq", pairs)


def attention_body(blocks, heads, *refs):
    query_ref, block_refs, out_ref = refs[0], refs[1 : 1 + blocks], refs[1 + blocks]
    rank = lax.axis_index("seq")
    inside = jnp.logical_and(rank > 0, rank < lax.axis_size("seq") - 1)
    bias = jnp.where(inside, 0.0, masked_score).astype(jnp.float32)
    scale = math.log2(math.e) / math.sqrt(HD)

    def scores_of(head):
        query = query_ref[:, head * HD : (head + 1) * HD]
        scores = [
            lax.dot_general(
                query, ref[0], (((1,), (1,)), ((), ())), preferred_element_type=jnp.float32
            )
            for ref in block_refs
        ]
        scores[-1] = scores[-1] + bias
        return scores

    scores = scores_of(0)
    for head in range(heads):
        later = scores_of(head + 1) if head + 1 < heads else None
        peak = jnp.max(functools.reduce(jnp.maximum, scores), axis=1, keepdims=True) * scale
        weights = [jnp.exp2(part * scale - peak) for part in scores]
        weight_sum = jnp.sum(functools.reduce(jnp.add, weights), axis=1, keepdims=True)
        numerator = functools.reduce(
            jnp.add,
            [
                jnp.dot(part.astype(jnp.bfloat16), ref[1], preferred_element_type=jnp.float32)
                for part, ref in zip(weights, block_refs)
            ],
        )
        out_ref[:, head * HD : (head + 1) * HD] = (numerator / weight_sum).astype(jnp.bfloat16)
        scores = later


def attend(queries, pieces):
    blocks, (rows, width) = len(pieces), queries.shape
    pairs = rows * blocks * BLK * (width // HD)
    return call_kernel(
        functools.partial(attention_body, blocks, width // HD),
        jax.ShapeDtypeStruct(queries.shape, jnp.bfloat16),
        [queries, *pieces],
        flops=4 * pairs * HD,
        moved=4 * queries.size + 2 * blocks * pieces[0].size,
        transcendentals=pairs,
    )


def exchange_blocks(rows):
    count = lax.axis_size("seq")
    bits = count.bit_length() - 1
    outer = [(i, i + 1) for i in range(1, count - 1, 2)]
    outer = outer + [(j, i) for i, j in outer]
    far = [flip(rows, 1 << bit) for bit in range(bits - 1, 1, -1)]
    beside = lax.ppermute(rows, "seq", outer)
    return [rows, flip(rows, 1), flip(rows, 2)] + far + [beside]


def after(value, earlier):
    return lax.optimization_barrier((value, earlier))[0]


class Ring:
    def __init__(self):
        self.count = lax.axis_size("seq")
        self.layers = self.count // 4
        self.chips = self.count // 2

    def place(self, index):
        layer = jnp.where(index < self.layers, index, self.chips - 1 - index)
        return layer, (index >= self.layers).astype(jnp.int32)

    def index(self):
        rank = lax.axis_index("seq")
        layer = rank // 4
        return jnp.where(rank // 2 % 2 == 0, layer, self.chips - 1 - layer)

    def shift(self, value, step):
        def rank_of(index):
            index = index % self.chips
            return 4 * index if index < self.layers else 4 * (self.chips - 1 - index) + 2

        pairs = [
            (rank_of(index) + core, rank_of(index + step) + core)
            for index in range(self.chips)
            for core in (0, 1)
        ]
        return lax.ppermute(value, "seq", pairs)

    def offsets(self):
        steps = [0]
        for step in range(1, self.chips // 2):
            steps += [step, -step]
        return steps + [self.chips // 2]

    def side_and_slot(self, offset):
        layer, across = self.place(lax.rem(self.index() + offset + self.chips, self.chips))
        per_side = self.layers // 2
        return layer // per_side, 2 * lax.rem(layer, per_side) + across

    def ranks(self, side, offsets):
        before, answer = jnp.int32(0), []
        for offset in offsets:
            belongs = self.side_and_slot(offset)[0] == side
            answer.append((belongs, before))
            before = before + belongs.astype(jnp.int32)
        return answer


def hold(held, slot, same_ref, other_ref):
    step = same_ref.shape[0]
    core = lax.axis_index("seq") % 2
    for where, ref in ((core, same_ref), (1 - core, other_ref)):
        held[pl.ds(pl.multiple_of((2 * slot + where) * step, 16), step), :] = ref[...]


def times(rows_ref, weight):
    return lax.dot_general(
        rows_ref[...], weight, (((1,), (1,)), ((), ())), preferred_element_type=jnp.float32
    )


def sent_body(first, width, offsets, *refs):
    rows_ref, same_refs = refs[0], refs[1 : 1 + len(offsets)]
    other_refs, (out_ref, held) = refs[1 + len(offsets) : 1 + 2 * len(offsets)], refs[-2:]
    ring = Ring()
    ranks = ring.ranks(1 - lax.axis_index("head"), offsets)
    for (belongs, rank), same_ref, other_ref in zip(ranks, same_refs, other_refs):
        for slot in range(width):

            @pl.when(jnp.logical_and(belongs, rank == first + slot))
            def _():
                hold(held, slot, same_ref, other_ref)

    out_ref[...] = times(rows_ref, held[...]).astype(jnp.bfloat16)


def sent(attended, first, width, offsets, same, other):
    step, depth = same[0].shape
    columns = 2 * width * step
    return call_kernel(
        functools.partial(sent_body, first, width, offsets),
        jax.ShapeDtypeStruct((attended.shape[0], columns), jnp.bfloat16),
        [attended, *same[: len(offsets)], *other[: len(offsets)]],
        scratch=[pltpu.VMEM((columns, depth), jnp.bfloat16)],
        flops=2 * attended.size * columns,
        moved=2 * columns * (attended.shape[0] + depth),
    )


def kept_body(offsets, *refs):
    rows_ref, same_refs = refs[0], refs[1 : 1 + len(offsets)]
    other_refs, (out_ref, held) = refs[1 + len(offsets) : 1 + 2 * len(offsets)], refs[-2:]
    ring, head = Ring(), lax.axis_index("head")
    for offset, same_ref, other_ref in zip(offsets, same_refs, other_refs):
        side, slot = ring.side_and_slot(offset)

        @pl.when(side == head)
        def _():
            hold(held, slot, same_ref, other_ref)

    slots, _, columns = out_ref.shape
    for slot in range(slots):
        out_ref[slot] = times(rows_ref, held[slot * columns : (slot + 1) * columns, :])


def kept(attended, offsets, same, other):
    (step, depth), slots = same[0].shape, len(offsets) // 2
    return call_kernel(
        functools.partial(kept_body, offsets),
        jax.ShapeDtypeStruct((slots, attended.shape[0], 2 * step), jnp.float32),
        [attended, *same, *other],
        scratch=[pltpu.VMEM((2 * slots * step, depth), jnp.bfloat16)],
        flops=4 * attended.size * slots * step,
        moved=4 * slots * step * (2 * attended.shape[0] + depth),
    )


def total_body(offsets, widths, *refs):
    kept_ref, received, out_ref = refs[0], refs[1:-1], refs[-1]
    ring = Ring()
    slots, _, columns = kept_ref.shape
    ranks = ring.ranks(lax.axis_index("head"), offsets)
    placed = [(ref, at) for ref, width in zip(received, widths) for at in range(width)]
    slot_of = [jnp.int32(0)] * len(placed)
    for offset, (belongs, rank) in zip(offsets, ranks):
        slot = ring.side_and_slot(offset)[1]
        for entry in range(len(placed)):
            here = jnp.logical_and(belongs, rank == entry)
            slot_of[entry] = jnp.where(here, slot, slot_of[entry])
    for slot in range(slots):
        for entry, (ref, at) in enumerate(placed):

            @pl.when(slot_of[entry] == slot)
            def _():
                there = ref[:, at * columns : (at + 1) * columns].astype(jnp.float32)
                out_ref[:, slot * columns : (slot + 1) * columns] = (kept_ref[slot] + there).astype(
                    jnp.bfloat16
                )


def total(kept_terms, received, widths, offsets):
    slots, rows, columns = kept_terms.shape
    return call_kernel(
        functools.partial(total_body, offsets, widths),
        jax.ShapeDtypeStruct((rows, slots * columns), jnp.bfloat16),
        [kept_terms, *received],
        moved=8 * kept_terms.size,
    )


def project_on_ring(queries, kv, out_weight):
    ring = Ring()
    shard = out_weight.T
    half = shard.shape[0] // 2

    def swap(value):
        return lax.ppermute(value, "head", [(0, 1), (1, 0)])

    def both_ways(onward, back):
        return ring.shift(onward, -1), ring.shift(back, 1)

    offsets = ring.offsets()
    same = [shard]
    pieces = exchange_blocks(kv)
    tied = (1, 2, 3, 4, 5)
    tied_pieces = [pieces[i] for i in tied]
    shard, tied_pieces = lax.optimization_barrier((shard, tied_pieces))
    for i, piece in zip(tied, tied_pieces):
        pieces[i] = piece
    first_pair = both_ways(shard, shard)
    attended = attend(queries, pieces)
    first_pair, attended = lax.optimization_barrier((first_pair, attended))
    second_pair = both_ways(*first_pair)
    third_pair = both_ways(*second_pair)
    same = [shard, *first_pair, *second_pair, *third_pair]
    other = [flip(value, 1) for value in same]
    first = swap(sent(attended, 0, 1, offsets[:5], same, other))
    third_pair, first = lax.optimization_barrier((third_pair, first))
    opposite = both_ways(third_pair[0][:half], third_pair[1][half:])
    same.append(jnp.concatenate(opposite, axis=0))
    other.append(flip(same[-1], 1))
    widths = (1, 2, 1)
    second = swap(sent(attended, 1, 2, offsets[:7], same, other))
    third = swap(sent(attended, 3, 1, offsets, same, other))
    terms = kept(attended, offsets, same, other)
    return total(terms, [first, second, third], widths, offsets)


def project_gathered(attended, out_weight):
    terms = jnp.dot(
        attended,
        lax.all_gather(out_weight, "seq", axis=1, tiled=True),
        preferred_element_type=jnp.float32,
    )
    return lax.psum_scatter(terms.astype(jnp.bfloat16), "head", scatter_dimension=1, tiled=True)


def local(queries, key_rows, value_rows, out_weight):
    kv = jnp.stack([key_rows, value_rows])
    chips = lax.axis_size("seq") // 2
    if chips == 8 and lax.axis_size("head") == 2 and out_weight.shape[1] % 32 == 0:
        return project_on_ring(queries, kv, out_weight)
    attended = attend(queries, exchange_blocks(kv))
    return project_gathered(attended, out_weight)


def solution(mesh):
    in_specs = (P("seq", "head"), P("seq", "head"), P("seq", "head"), P("head", "seq"))
    out_specs = P("seq", "head")
    return jax.shard_map(local, mesh=mesh, in_specs=in_specs, out_specs=out_specs, check_vma=False)
```

```python
import functools
import math

import jax
import jax.numpy as jnp
from jax import lax
from jax.experimental import pallas as pl
from jax.experimental.pallas import tpu as pltpu
from jax.sharding import PartitionSpec as P

HD = 128
BLK = 256

masked_score = -1e30
vmem_limit = 20 * 2**20
in_vmem = pl.BlockSpec(memory_space=pltpu.VMEM)


def call_kernel(body, out_shape, operands, scratch=()):
    many = isinstance(out_shape, (list, tuple))
    return pl.pallas_call(
        body,
        out_shape=out_shape,
        in_specs=[in_vmem] * len(operands),
        out_specs=[in_vmem] * len(out_shape) if many else in_vmem,
        scratch_shapes=list(scratch),
        compiler_params=pltpu.CompilerParams(vmem_limit_bytes=vmem_limit),
        cost_estimate=pl.CostEstimate(flops=1, bytes_accessed=1, transcendentals=0),
    )(*operands)


def flip(value, mask):
    pairs = [(source, source ^ mask) for source in range(lax.axis_size("seq"))]
    return lax.ppermute(value, "seq", pairs)


def attention_body(blocks, heads, *refs):
    query_ref, block_refs, out_ref = refs[0], refs[1 : 1 + blocks], refs[1 + blocks]
    rank = lax.axis_index("seq")
    inside = jnp.logical_and(rank > 0, rank < lax.axis_size("seq") - 1)
    bias = jnp.where(inside, 0.0, masked_score).astype(jnp.float32)
    scale = math.log2(math.e) / math.sqrt(HD)

    def scores_of(head):
        query = query_ref[:, head * HD : (head + 1) * HD]
        scores = [
            lax.dot_general(
                query, ref[0], (((1,), (1,)), ((), ())), preferred_element_type=jnp.float32
            )
            for ref in block_refs
        ]
        scores[-1] = scores[-1] + bias
        return scores

    scores = scores_of(0)
    for head in range(heads):
        later = scores_of(head + 1) if head + 1 < heads else None
        peak = jnp.max(functools.reduce(jnp.maximum, scores), axis=1, keepdims=True) * scale
        weights = [jnp.exp2(part * scale - peak) for part in scores]
        weight_sum = jnp.sum(functools.reduce(jnp.add, weights), axis=1, keepdims=True)
        numerator = functools.reduce(
            jnp.add,
            [
                jnp.dot(part.astype(jnp.bfloat16), ref[1], preferred_element_type=jnp.float32)
                for part, ref in zip(weights, block_refs)
            ],
        )
        out_ref[:, head * HD : (head + 1) * HD] = (numerator / weight_sum).astype(jnp.bfloat16)
        scores = later


def attend(queries, pieces):
    blocks, width = len(pieces), queries.shape[1]
    return call_kernel(
        functools.partial(attention_body, blocks, width // HD),
        jax.ShapeDtypeStruct(queries.shape, jnp.bfloat16),
        [queries, *pieces],
    )


def exchange_blocks(rows):
    count = lax.axis_size("seq")
    bits = count.bit_length() - 1
    outer = [(i, i + 1) for i in range(1, count - 1, 2)]
    outer = outer + [(j, i) for i, j in outer]
    far = [flip(rows, 1 << bit) for bit in range(bits - 1, 0, -1)]
    rows = after(rows, far[-1])
    return [rows] + far + [flip(rows, 1), lax.ppermute(rows, "seq", outer)]


def after(value, earlier):
    return lax.optimization_barrier((value, earlier))[0]


class Ring:
    def __init__(self):
        self.count = lax.axis_size("seq")
        self.layers = self.count // 4
        self.chips = self.count // 2

    def place(self, index):
        layer = jnp.where(index < self.layers, index, self.chips - 1 - index)
        return layer, (index >= self.layers).astype(jnp.int32)

    def index(self):
        rank = lax.axis_index("seq")
        layer = rank // 4
        return jnp.where(rank // 2 % 2 == 0, layer, self.chips - 1 - layer)

    def shift(self, value, step):
        def rank_of(index):
            index = index % self.chips
            return 4 * index if index < self.layers else 4 * (self.chips - 1 - index) + 2

        pairs = [
            (rank_of(index) + core, rank_of(index + step) + core)
            for index in range(self.chips)
            for core in (0, 1)
        ]
        return lax.ppermute(value, "seq", pairs)

    def offsets(self):
        steps = [0]
        for step in range(1, self.chips // 2):
            steps += [step, -step]
        return steps + [self.chips // 2]

    def side_and_slot(self, offset):
        layer, across = self.place(lax.rem(self.index() + offset + self.chips, self.chips))
        per_side = self.layers // 2
        return layer // per_side, 2 * lax.rem(layer, per_side) + across

    def ranks(self, side, offsets):
        before, answer = jnp.int32(0), []
        for offset in offsets:
            belongs = self.side_and_slot(offset)[0] == side
            answer.append((belongs, before))
            before = before + belongs.astype(jnp.int32)
        return answer


def hold(held, slot, ref):
    step = ref.shape[0]
    held[pl.ds(pl.multiple_of(slot * step, 16), step), :] = ref[...]


def times(weight, rows_ref):
    return lax.dot_general(
        weight, rows_ref[...], (((1,), (1,)), ((), ())), preferred_element_type=jnp.float32
    )


def sent_body(first, width, offsets, *refs):
    (mine_ref, theirs_ref), parts = refs[:2], refs[2 : 2 + len(offsets)]
    to_same_ref, to_other_ref, held = refs[2 + len(offsets) :]
    ranks = Ring().ranks(1 - lax.axis_index("head"), offsets)
    for (belongs, rank), ref in zip(ranks, parts):
        for slot in range(width):

            @pl.when(jnp.logical_and(belongs, rank == first + slot))
            def _():
                hold(held, slot, ref)

    to_same_ref[...] = times(held[...], mine_ref).astype(jnp.bfloat16)
    to_other_ref[...] = times(held[...], theirs_ref).astype(jnp.bfloat16)


def sent(rows, first, width, offsets, parts):
    step, depth = parts[0].shape
    shape = jax.ShapeDtypeStruct((width * step, rows[0].shape[0]), jnp.bfloat16)
    return call_kernel(
        functools.partial(sent_body, first, width, offsets),
        [shape, shape],
        [*rows, *parts[: len(offsets)]],
        scratch=[pltpu.VMEM((width * step, depth), jnp.bfloat16)],
    )


def kept_body(offsets, *refs):
    (mine_ref, theirs_ref), parts = refs[:2], refs[2 : 2 + len(offsets)]
    keep_ref, to_core_ref, held = refs[2 + len(offsets) :]
    ring, head = Ring(), lax.axis_index("head")
    for offset, ref in zip(offsets, parts):
        side, slot = ring.side_and_slot(offset)

        @pl.when(side == head)
        def _():
            hold(held, slot, ref)

    keep_ref[...] = times(held[...], mine_ref)
    to_core_ref[...] = times(held[...], theirs_ref).astype(jnp.bfloat16)


def kept(rows, offsets, parts):
    step, depth = parts[0].shape
    shape = (step * len(offsets) // 2, rows[0].shape[0])
    return call_kernel(
        functools.partial(kept_body, offsets),
        [jax.ShapeDtypeStruct(shape, jnp.float32), jax.ShapeDtypeStruct(shape, jnp.bfloat16)],
        [*rows, *parts],
        scratch=[pltpu.VMEM((shape[0], depth), jnp.bfloat16)],
    )


def total_body(offsets, widths, *refs):
    keep_ref, from_core_ref, received, out_ref, turned = refs[0], refs[1], refs[2:-2], *refs[-2:]
    ring = Ring()
    slots = len(offsets) // 2
    step = keep_ref.shape[0] // slots
    core = lax.axis_index("seq") % 2
    ranks = ring.ranks(lax.axis_index("head"), offsets)
    entry = 0
    for same_ref, other_ref, width in zip(received[0::2], received[1::2], widths):
        for at in range(width):
            slot = jnp.int32(0)
            for offset, (belongs, rank) in zip(offsets, ranks):
                here = jnp.logical_and(belongs, rank == entry)
                slot = jnp.where(here, ring.side_and_slot(offset)[1], slot)
            entry += 1
            rows = pl.ds(pl.multiple_of(slot * step, 16), step)
            there = slice(at * step, (at + 1) * step)
            for where, kept_ref, ref in (
                (core, keep_ref, same_ref),
                (1 - core, from_core_ref, other_ref),
            ):
                both = kept_ref[rows, :].astype(jnp.float32) + ref[there, :].astype(jnp.float32)
                start = pl.multiple_of((2 * slot + where) * step, 16)
                turned[pl.ds(start, step), :] = both.astype(jnp.bfloat16)
    tokens = keep_ref.shape[1]
    row = lax.broadcasted_iota(jnp.int32, (tokens, tokens), 0)
    column = lax.broadcasted_iota(jnp.int32, (tokens, tokens), 1)
    identity = jnp.where(row == column, 1.0, 0.0).astype(jnp.bfloat16)
    out_ref[...] = times(identity, turned).astype(jnp.bfloat16)


def total(keep, from_core, received, widths, offsets):
    columns, rows = keep.shape
    return call_kernel(
        functools.partial(total_body, offsets, widths),
        jax.ShapeDtypeStruct((rows, 2 * columns), jnp.bfloat16),
        [keep, from_core, *received],
        scratch=[pltpu.VMEM((2 * columns, rows), jnp.bfloat16)],
    )


def project_on_ring(queries, kv, out_weight):
    ring = Ring()
    shard = out_weight.T
    half = shard.shape[0] // 2
    count = lax.axis_size("seq")
    offsets, widths = ring.offsets(), (1, 2, 1)

    def both_ways(onward, back):
        return [ring.shift(onward, -1), ring.shift(back, 1)]

    def swap(products):
        same, other = products
        crossed = [(2 * i + h, 2 * (i ^ 1) + 1 - h) for i in range(count) for h in range(2)]
        return [
            lax.ppermute(same, "head", [(0, 1), (1, 0)]),
            lax.ppermute(other, ("seq", "head"), crossed),
        ]

    pair = both_ways(shard, shard)
    parts = [shard, *pair]
    pieces = exchange_blocks(kv)
    pair, pieces[1:] = lax.optimization_barrier((pair, pieces[1:]))
    pair = both_ways(*pair)
    parts += pair
    attended = attend(queries, pieces)
    rows = [attended, flip(attended, 1)]
    first = swap(sent(rows, 0, 1, offsets[:5], parts))
    pair, attended = lax.optimization_barrier((pair, attended))
    rows[0] = attended
    pair = both_ways(*pair)
    parts += pair
    second = swap(sent(rows, 1, 2, offsets[:7], parts))
    pair, first = lax.optimization_barrier((pair, first))
    opposite = both_ways(pair[0][:half], pair[1][half:])
    parts.append(jnp.concatenate(opposite, axis=0))
    parts[-1], second = lax.optimization_barrier((parts[-1], second))
    product = sent(rows, 3, 1, offsets, parts)
    rows[0], product = lax.optimization_barrier((rows[0], product))
    third = swap(product)
    keep, to_core = kept(rows, offsets, parts)
    return total(keep, flip(to_core, 1), [*first, *second, *third], widths, offsets)


def project_gathered(attended, out_weight):
    terms = jnp.dot(
        attended,
        lax.all_gather(out_weight, "seq", axis=1, tiled=True),
        preferred_element_type=jnp.float32,
    )
    return lax.psum_scatter(terms.astype(jnp.bfloat16), "head", scatter_dimension=1, tiled=True)


def local(queries, key_rows, value_rows, out_weight):
    kv = jnp.stack([key_rows, value_rows])
    chips = lax.axis_size("seq") // 2
    if chips == 8 and lax.axis_size("head") == 2 and out_weight.shape[1] % 32 == 0:
        return project_on_ring(queries, kv, out_weight)
    attended = attend(queries, exchange_blocks(kv))
    return project_gathered(attended, out_weight)


def solution(mesh):
    in_specs = (P("seq", "head"), P("seq", "head"), P("seq", "head"), P("head", "seq"))
    out_specs = P("seq", "head")
    return jax.shard_map(local, mesh=mesh, in_specs=in_specs, out_specs=out_specs, check_vma=False)
```

```python
import functools
import math

import jax
import jax.numpy as jnp
from jax import lax
from jax.experimental import pallas as pl
from jax.experimental.pallas import tpu as pltpu
from jax.sharding import PartitionSpec as P

HD = 128
BLK = 256

masked_score = -1e30
vmem_limit = 20 * 2**20
in_vmem = pl.BlockSpec(memory_space=pltpu.VMEM)


def call_kernel(body, out_shape, operands, scratch=()):
    many = isinstance(out_shape, (list, tuple))
    return pl.pallas_call(
        body,
        out_shape=out_shape,
        in_specs=[in_vmem] * len(operands),
        out_specs=[in_vmem] * len(out_shape) if many else in_vmem,
        scratch_shapes=list(scratch),
        compiler_params=pltpu.CompilerParams(vmem_limit_bytes=vmem_limit),
        cost_estimate=pl.CostEstimate(flops=1, bytes_accessed=1, transcendentals=0),
    )(*operands)


def flip(value, mask):
    pairs = [(source, source ^ mask) for source in range(lax.axis_size("seq"))]
    return lax.ppermute(value, "seq", pairs)


def attention_body(blocks, heads, *refs):
    query_ref, block_refs, out_ref = refs[0], refs[1 : 1 + blocks], refs[1 + blocks]
    rank = lax.axis_index("seq")
    inside = jnp.logical_and(rank > 0, rank < lax.axis_size("seq") - 1)
    bias = jnp.where(inside, 0.0, masked_score).astype(jnp.float32)
    scale = math.log2(math.e) / math.sqrt(HD)

    def scores_of(head):
        query = query_ref[:, head * HD : (head + 1) * HD]
        scores = [
            lax.dot_general(
                query, ref[0], (((1,), (1,)), ((), ())), preferred_element_type=jnp.float32
            )
            for ref in block_refs
        ]
        scores[-1] = scores[-1] + bias
        return scores

    scores = scores_of(0)
    for head in range(heads):
        later = scores_of(head + 1) if head + 1 < heads else None
        peak = jnp.max(functools.reduce(jnp.maximum, scores), axis=1, keepdims=True) * scale
        weights = [jnp.exp2(part * scale - peak) for part in scores]
        weight_sum = jnp.sum(functools.reduce(jnp.add, weights), axis=1, keepdims=True)
        numerator = functools.reduce(
            jnp.add,
            [
                jnp.dot(part.astype(jnp.bfloat16), ref[1], preferred_element_type=jnp.float32)
                for part, ref in zip(weights, block_refs)
            ],
        )
        out_ref[:, head * HD : (head + 1) * HD] = (numerator / weight_sum).astype(jnp.bfloat16)
        scores = later


def attend(queries, pieces):
    blocks, width = len(pieces), queries.shape[1]
    return call_kernel(
        functools.partial(attention_body, blocks, width // HD),
        jax.ShapeDtypeStruct(queries.shape, jnp.bfloat16),
        [queries, *pieces],
    )


def staged_body(from_ref, to_ref):
    to_ref[...] = from_ref[...]


def staged(value):
    shape = jax.ShapeDtypeStruct(value.shape, value.dtype)
    return call_kernel(staged_body, shape, [value])


def exchange_blocks(rows, early=()):
    count = lax.axis_size("seq")
    bits = count.bit_length() - 1
    outer = [(i, i + 1) for i in range(1, count - 1, 2)]
    outer = outer + [(j, i) for i, j in outer]
    far = [flip(rows, 1 << bit) for bit in range(bits - 1, 1, -1)]
    beside = lax.ppermute(rows, "seq", outer)
    rows = after(rows, (far[-1], early))
    return [rows, flip(rows, 1), flip(rows, 2)] + far + [beside]


def after(value, earlier):
    return lax.optimization_barrier((value, earlier))[0]


class Ring:
    def __init__(self):
        self.count = lax.axis_size("seq")
        self.layers = self.count // 4
        self.chips = self.count // 2

    def place(self, index):
        layer = jnp.where(index < self.layers, index, self.chips - 1 - index)
        return layer, (index >= self.layers).astype(jnp.int32)

    def index(self):
        rank = lax.axis_index("seq")
        layer = rank // 4
        return jnp.where(rank // 2 % 2 == 0, layer, self.chips - 1 - layer)

    def shift(self, value, step):
        def rank_of(index):
            index = index % self.chips
            return 4 * index if index < self.layers else 4 * (self.chips - 1 - index) + 2

        pairs = [
            (rank_of(index) + core, rank_of(index + step) + core)
            for index in range(self.chips)
            for core in (0, 1)
        ]
        return lax.ppermute(value, "seq", pairs)

    def offsets(self):
        steps = [0]
        for step in range(1, self.chips // 2):
            steps += [step, -step]
        return steps + [self.chips // 2]

    def side_and_slot(self, offset):
        layer, across = self.place(lax.rem(self.index() + offset + self.chips, self.chips))
        per_side = self.layers // 2
        return layer // per_side, 2 * lax.rem(layer, per_side) + across

    def ranks(self, side, offsets):
        before, answer = jnp.int32(0), []
        for offset in offsets:
            belongs = self.side_and_slot(offset)[0] == side
            answer.append((belongs, before))
            before = before + belongs.astype(jnp.int32)
        return answer


def hold(held, start, refs):
    for ref in refs:
        held[pl.ds(pl.multiple_of(start, 16), ref.shape[0]), :] = ref[...]
        start = start + ref.shape[0]


def grouped(refs, offsets):
    return [refs[at : at + 1] if at < len(offsets) - 1 else refs[at:] for at in range(len(offsets))]


def times(weight, rows_ref):
    return lax.dot_general(
        weight, rows_ref[...], (((1,), (1,)), ((), ())), preferred_element_type=jnp.float32
    )


def sent_body(first, width, offsets, *refs):
    (mine_ref, theirs_ref), parts = refs[:2], grouped(refs[2:-3], offsets)
    to_same_ref, to_other_ref, held = refs[-3:]
    step = held.shape[0] // width
    ranks = Ring().ranks(1 - lax.axis_index("head"), offsets)
    for (belongs, rank), part in zip(ranks, parts):
        for slot in range(width):

            @pl.when(jnp.logical_and(belongs, rank == first + slot))
            def _():
                hold(held, slot * step, part)

    to_same_ref[...] = times(held[...], mine_ref).astype(jnp.bfloat16)
    to_other_ref[...] = times(held[...], theirs_ref).astype(jnp.bfloat16)


def sent(rows, first, width, offsets, parts):
    step, depth = parts[0].shape
    shape = jax.ShapeDtypeStruct((width * step, rows[0].shape[0]), jnp.bfloat16)
    return call_kernel(
        functools.partial(sent_body, first, width, offsets),
        [shape, shape],
        [*rows, *parts],
        scratch=[pltpu.VMEM((width * step, depth), jnp.bfloat16)],
    )


def kept_body(offsets, *refs):
    rows_ref, parts, (out_ref, held) = refs[0], grouped(refs[1:-2], offsets), refs[-2:]
    step = 2 * held.shape[0] // len(offsets)
    ring, head = Ring(), lax.axis_index("head")
    for offset, part in zip(offsets, parts):
        side, slot = ring.side_and_slot(offset)

        @pl.when(side == head)
        def _():
            hold(held, slot * step, part)

    out_ref[...] = times(held[...], rows_ref).astype(out_ref.dtype)


def kept(rows, offsets, parts, dtype):
    step, depth = parts[0].shape
    shape = (step * len(offsets) // 2, rows.shape[0])
    return call_kernel(
        functools.partial(kept_body, offsets),
        jax.ShapeDtypeStruct(shape, dtype),
        [rows, *parts],
        scratch=[pltpu.VMEM((shape[0], depth), jnp.bfloat16)],
    )


def total_body(offsets, widths, first, *refs):
    ring = Ring()
    keep_ref, from_core_ref = refs[:2]
    (*received, out_ref, turned) = refs[2:]
    done_ref = received.pop(0) if first else None
    slots = len(offsets) // 2
    step = keep_ref.shape[0] // slots
    core = lax.axis_index("seq") % 2
    ranks = ring.ranks(lax.axis_index("head"), offsets)
    tokens = keep_ref.shape[1]
    row = lax.broadcasted_iota(jnp.int32, (tokens, tokens), 0)
    column = lax.broadcasted_iota(jnp.int32, (tokens, tokens), 1)
    identity = jnp.where(row == column, 1.0, 0.0).astype(jnp.bfloat16)
    if not first:
        turned[...] = jnp.zeros(turned.shape, turned.dtype)
    entry, slot = first, None
    for same_ref, other_ref, width in zip(received[0::2], received[1::2], widths):
        for at in range(width):
            slot = jnp.int32(0)
            for offset, (belongs, rank) in zip(offsets, ranks):
                here = jnp.logical_and(belongs, rank == entry)
                slot = jnp.where(here, ring.side_and_slot(offset)[1], slot)
            entry += 1
            rows = pl.ds(pl.multiple_of(slot * step, 16), step)
            there = slice(at * step, (at + 1) * step)
            for where, kept_ref, ref in (
                (core, keep_ref, same_ref),
                (1 - core, from_core_ref, other_ref),
            ):
                both = kept_ref[rows, :].astype(jnp.float32) + ref[there, :].astype(jnp.float32)
                start = where * step if first else (2 * slot + where) * step
                turned[pl.ds(pl.multiple_of(start, 16), step), :] = both.astype(jnp.bfloat16)
    values = times(identity, turned).astype(jnp.bfloat16)
    if not first:
        out_ref[...] = values
        return
    out_ref[...] = done_ref[...]
    for at in range(slots):

        @pl.when(slot == at)
        def _():
            out_ref[:, 2 * at * step : 2 * (at + 1) * step] = values


def total(keep, from_core, received, widths, offsets, done=None):
    columns, rows = keep.shape
    first = 0 if done is None else len(offsets) // 2 - sum(widths)
    held = 2 * columns if done is None else 4 * columns // len(offsets)
    return call_kernel(
        functools.partial(total_body, offsets, widths, first),
        jax.ShapeDtypeStruct((rows, 2 * columns), jnp.bfloat16),
        [keep, from_core, *([] if done is None else [done]), *received],
        scratch=[pltpu.VMEM((held, rows), jnp.bfloat16)],
    )


def project_on_ring(queries, kv, out_weight):
    ring = Ring()
    shard = out_weight.T
    half = shard.shape[0] // 2
    count = lax.axis_size("seq")
    offsets, widths = ring.offsets(), (1, 2, 1)

    def both_ways(onward, back):
        return [ring.shift(onward, -1), ring.shift(back, 1)]

    def swap(products):
        same, other = products
        crossed = [(2 * i + h, 2 * (i ^ 1) + 1 - h) for i in range(count) for h in range(2)]
        return [
            lax.ppermute(same, "head", [(0, 1), (1, 0)]),
            lax.ppermute(other, ("seq", "head"), crossed),
        ]

    pair = both_ways(shard, shard)
    parts = [shard, *pair]
    queries = staged(queries)
    pieces = exchange_blocks(kv, queries)
    pair, pieces[1:] = lax.optimization_barrier((pair, pieces[1:]))
    pair = both_ways(*pair)
    parts += pair
    attended = attend(queries, pieces)
    rows = [attended, flip(attended, 1)]
    first = swap(sent(rows, 0, 1, offsets[:5], parts))
    pair, attended = lax.optimization_barrier((pair, attended))
    rows[0] = attended
    pair = both_ways(*pair)
    parts += pair
    product = sent(rows, 1, 2, offsets[:7], parts)
    pair, first, product = lax.optimization_barrier((pair, first, product))
    second = swap(product)
    opposite = both_ways(pair[0][:half], pair[1][half:])
    parts += opposite
    parts[-2:], second = lax.optimization_barrier((parts[-2:], second))
    product = sent(rows, 3, 1, offsets, parts)
    rows, product = lax.optimization_barrier((rows, product))
    third = swap(product)
    to_core = kept(rows[1], offsets, parts, jnp.bfloat16)
    keep = kept(rows[0], offsets, parts, jnp.float32)
    from_core = flip(to_core, 1)
    done = total(keep, from_core, [*first, *second], widths[:2], offsets)
    return total(keep, from_core, third, widths[2:], offsets, done)


def project_gathered(attended, out_weight):
    terms = jnp.dot(
        attended,
        lax.all_gather(out_weight, "seq", axis=1, tiled=True),
        preferred_element_type=jnp.float32,
    )
    return lax.psum_scatter(terms.astype(jnp.bfloat16), "head", scatter_dimension=1, tiled=True)


def local(queries, key_rows, value_rows, out_weight):
    kv = jnp.stack([key_rows, value_rows])
    chips = lax.axis_size("seq") // 2
    if chips == 8 and lax.axis_size("head") == 2 and out_weight.shape[1] % 32 == 0:
        return project_on_ring(queries, kv, out_weight)
    attended = attend(queries, exchange_blocks(kv))
    return project_gathered(attended, out_weight)


def solution(mesh):
    in_specs = (P("seq", "head"), P("seq", "head"), P("seq", "head"), P("head", "seq"))
    out_specs = P("seq", "head")
    return jax.shard_map(local, mesh=mesh, in_specs=in_specs, out_specs=out_specs, check_vma=False)
```

```python
import functools
import math

import jax
import jax.numpy as jnp
from jax import lax
from jax.experimental import pallas as pl
from jax.experimental.pallas import tpu as pltpu
from jax.sharding import PartitionSpec as P

HD = 128
BLK = 256

masked_score = -1e30
vmem_limit = 20 * 2**20
in_vmem = pl.BlockSpec(memory_space=pltpu.VMEM)


def call_kernel(body, out_shape, operands, scratch=()):
    many = isinstance(out_shape, (list, tuple))
    return pl.pallas_call(
        body,
        out_shape=out_shape,
        in_specs=[in_vmem] * len(operands),
        out_specs=[in_vmem] * len(out_shape) if many else in_vmem,
        scratch_shapes=list(scratch),
        compiler_params=pltpu.CompilerParams(vmem_limit_bytes=vmem_limit),
        cost_estimate=pl.CostEstimate(flops=1, bytes_accessed=1, transcendentals=0),
    )(*operands)


def flip(value, mask):
    pairs = [(source, source ^ mask) for source in range(lax.axis_size("seq"))]
    return lax.ppermute(value, "seq", pairs)


def attention_body(blocks, heads, *refs):
    query_ref, block_refs, out_ref = refs[0], refs[1 : 1 + blocks], refs[1 + blocks]
    rank = lax.axis_index("seq")
    inside = jnp.logical_and(rank > 0, rank < lax.axis_size("seq") - 1)
    bias = jnp.where(inside, 0.0, masked_score).astype(jnp.float32)
    scale = math.log2(math.e) / math.sqrt(HD)

    def scores_of(head):
        query = query_ref[:, head * HD : (head + 1) * HD]
        scores = [
            lax.dot_general(
                query, ref[0], (((1,), (1,)), ((), ())), preferred_element_type=jnp.float32
            )
            for ref in block_refs
        ]
        scores[-1] = scores[-1] + bias
        return scores

    scores = scores_of(0)
    for head in range(heads):
        later = scores_of(head + 1) if head + 1 < heads else None
        peak = jnp.max(functools.reduce(jnp.maximum, scores), axis=1, keepdims=True) * scale
        weights = [jnp.exp2(part * scale - peak) for part in scores]
        weight_sum = jnp.sum(functools.reduce(jnp.add, weights), axis=1, keepdims=True)
        numerator = functools.reduce(
            jnp.add,
            [
                jnp.dot(part.astype(jnp.bfloat16), ref[1], preferred_element_type=jnp.float32)
                for part, ref in zip(weights, block_refs)
            ],
        )
        out_ref[:, head * HD : (head + 1) * HD] = (numerator / weight_sum).astype(jnp.bfloat16)
        scores = later


def attend(queries, pieces):
    blocks, width = len(pieces), queries.shape[1]
    return call_kernel(
        functools.partial(attention_body, blocks, width // HD),
        jax.ShapeDtypeStruct(queries.shape, jnp.bfloat16),
        [queries, *pieces],
    )


def staged_body(from_ref, to_ref):
    to_ref[...] = from_ref[...]


def staged(value):
    shape = jax.ShapeDtypeStruct(value.shape, value.dtype)
    return call_kernel(staged_body, shape, [value])


def exchange_blocks(rows, early=()):
    count = lax.axis_size("seq")
    bits = count.bit_length() - 1
    outer = [(i, i + 1) for i in range(1, count - 1, 2)]
    outer = outer + [(j, i) for i, j in outer]
    far = [flip(rows, 1 << bit) for bit in range(bits - 1, 1, -1)]
    beside = lax.ppermute(rows, "seq", outer)
    rows = after(rows, early)
    return [rows, flip(rows, 1), flip(rows, 2)] + far + [beside]


def after(value, earlier):
    return lax.optimization_barrier((value, earlier))[0]


class Ring:
    def __init__(self):
        self.count = lax.axis_size("seq")
        self.layers = self.count // 4
        self.chips = self.count // 2

    def place(self, index):
        layer = jnp.where(index < self.layers, index, self.chips - 1 - index)
        return layer, (index >= self.layers).astype(jnp.int32)

    def index(self):
        rank = lax.axis_index("seq")
        layer = rank // 4
        return jnp.where(rank // 2 % 2 == 0, layer, self.chips - 1 - layer)

    def shift(self, value, step):
        def rank_of(index):
            index = index % self.chips
            return 4 * index if index < self.layers else 4 * (self.chips - 1 - index) + 2

        pairs = [
            (rank_of(index) + core, rank_of(index + step) + core)
            for index in range(self.chips)
            for core in (0, 1)
        ]
        return lax.ppermute(value, "seq", pairs)

    def offsets(self):
        steps = [0]
        for step in range(1, self.chips // 2):
            steps += [step, -step]
        return steps + [self.chips // 2]

    def side_and_slot(self, offset):
        layer, across = self.place(lax.rem(self.index() + offset + self.chips, self.chips))
        per_side = self.layers // 2
        return layer // per_side, 2 * lax.rem(layer, per_side) + across

    def ranks(self, side, offsets):
        before, answer = jnp.int32(0), []
        for offset in offsets:
            belongs = self.side_and_slot(offset)[0] == side
            answer.append((belongs, before))
            before = before + belongs.astype(jnp.int32)
        return answer


def hold(held, start, refs):
    for ref in refs:
        held[pl.ds(pl.multiple_of(start, 16), ref.shape[0]), :] = ref[...]
        start = start + ref.shape[0]


def grouped(refs, offsets):
    return [refs[at : at + 1] if at < len(offsets) - 1 else refs[at:] for at in range(len(offsets))]


def times(weight, rows_ref):
    return lax.dot_general(
        weight, rows_ref[...], (((1,), (1,)), ((), ())), preferred_element_type=jnp.float32
    )


def sent_body(first, width, offsets, *refs):
    (mine_ref, theirs_ref), parts = refs[:2], grouped(refs[2:-3], offsets)
    to_same_ref, to_other_ref, held = refs[-3:]
    step = held.shape[0] // width
    ranks = Ring().ranks(1 - lax.axis_index("head"), offsets)
    for (belongs, rank), part in zip(ranks, parts):
        for slot in range(width):

            @pl.when(jnp.logical_and(belongs, rank == first + slot))
            def _():
                hold(held, slot * step, part)

    to_same_ref[...] = times(held[...], mine_ref).astype(jnp.bfloat16)
    to_other_ref[...] = times(held[...], theirs_ref).astype(jnp.bfloat16)


def sent(rows, first, width, offsets, parts):
    step, depth = parts[0].shape
    shape = jax.ShapeDtypeStruct((width * step, rows[0].shape[0]), jnp.bfloat16)
    return call_kernel(
        functools.partial(sent_body, first, width, offsets),
        [shape, shape],
        [*rows, *parts],
        scratch=[pltpu.VMEM((width * step, depth), jnp.bfloat16)],
    )


def kept_body(offsets, *refs):
    rows_ref, parts, (out_ref, held) = refs[0], grouped(refs[1:-2], offsets), refs[-2:]
    step = 2 * held.shape[0] // len(offsets)
    ring, head = Ring(), lax.axis_index("head")
    for offset, part in zip(offsets, parts):
        side, slot = ring.side_and_slot(offset)

        @pl.when(side == head)
        def _():
            hold(held, slot * step, part)

    out_ref[...] = times(held[...], rows_ref).astype(out_ref.dtype)


def kept(rows, offsets, parts, dtype):
    step, depth = parts[0].shape
    shape = (step * len(offsets) // 2, rows.shape[0])
    return call_kernel(
        functools.partial(kept_body, offsets),
        jax.ShapeDtypeStruct(shape, dtype),
        [rows, *parts],
        scratch=[pltpu.VMEM((shape[0], depth), jnp.bfloat16)],
    )


def total_body(offsets, widths, first, *refs):
    ring = Ring()
    keep_ref, from_core_ref = refs[:2]
    (*received, out_ref, turned) = refs[2:]
    done_ref = received.pop(0) if first else None
    slots = len(offsets) // 2
    step = keep_ref.shape[0] // slots
    core = lax.axis_index("seq") % 2
    ranks = ring.ranks(lax.axis_index("head"), offsets)
    tokens = keep_ref.shape[1]
    row = lax.broadcasted_iota(jnp.int32, (tokens, tokens), 0)
    column = lax.broadcasted_iota(jnp.int32, (tokens, tokens), 1)
    identity = jnp.where(row == column, 1.0, 0.0).astype(jnp.bfloat16)
    if not first:
        turned[...] = jnp.zeros(turned.shape, turned.dtype)
    entry, slot = first, None
    for same_ref, other_ref, width in zip(received[0::2], received[1::2], widths):
        for at in range(width):
            slot = jnp.int32(0)
            for offset, (belongs, rank) in zip(offsets, ranks):
                here = jnp.logical_and(belongs, rank == entry)
                slot = jnp.where(here, ring.side_and_slot(offset)[1], slot)
            entry += 1
            rows = pl.ds(pl.multiple_of(slot * step, 16), step)
            there = slice(at * step, (at + 1) * step)
            for where, kept_ref, ref in (
                (core, keep_ref, same_ref),
                (1 - core, from_core_ref, other_ref),
            ):
                both = kept_ref[rows, :].astype(jnp.float32) + ref[there, :].astype(jnp.float32)
                start = where * step if first else (2 * slot + where) * step
                turned[pl.ds(pl.multiple_of(start, 16), step), :] = both.astype(jnp.bfloat16)
    values = times(identity, turned).astype(jnp.bfloat16)
    if not first:
        out_ref[...] = values
        return
    out_ref[...] = done_ref[...]
    for at in range(slots):

        @pl.when(slot == at)
        def _():
            out_ref[:, 2 * at * step : 2 * (at + 1) * step] = values


def total(keep, from_core, received, widths, offsets, done=None):
    columns, rows = keep.shape
    first = 0 if done is None else len(offsets) // 2 - sum(widths)
    held = 2 * columns if done is None else 4 * columns // len(offsets)
    return call_kernel(
        functools.partial(total_body, offsets, widths, first),
        jax.ShapeDtypeStruct((rows, 2 * columns), jnp.bfloat16),
        [keep, from_core, *([] if done is None else [done]), *received],
        scratch=[pltpu.VMEM((held, rows), jnp.bfloat16)],
    )


def project_on_ring(queries, kv, out_weight):
    ring = Ring()
    shard = out_weight.T
    half = shard.shape[0] // 2
    count = lax.axis_size("seq")
    offsets, widths = ring.offsets(), (1, 2, 1)

    def both_ways(onward, back):
        return [ring.shift(onward, -1), ring.shift(back, 1)]

    def swap(products):
        same, other = products
        crossed = [(2 * i + h, 2 * (i ^ 1) + 1 - h) for i in range(count) for h in range(2)]
        return [
            lax.ppermute(same, "head", [(0, 1), (1, 0)]),
            lax.ppermute(other, ("seq", "head"), crossed),
        ]

    pair = both_ways(shard, shard)
    parts = [shard, *pair]
    queries = staged(queries)
    pieces = exchange_blocks(kv, (queries, pair[0]))
    pair, pieces[1:] = lax.optimization_barrier((pair, pieces[1:]))
    pair = both_ways(*pair)
    parts += pair
    attended = attend(queries, pieces)
    rows = [attended, flip(attended, 1)]
    first = swap(sent(rows, 0, 1, offsets[:5], parts))
    pair = [after(shard, attended) for shard in pair]
    pair = both_ways(*pair)
    parts += pair
    product = sent(rows, 1, 2, offsets[:7], parts)
    pair = [after(shard, (first, product)) for shard in pair]
    second = swap(product)
    opposite = both_ways(pair[0][:half], pair[1][half:])
    parts += opposite
    parts[-2:], second = lax.optimization_barrier((parts[-2:], second))
    product = sent(rows, 3, 1, offsets, parts)
    rows, product = lax.optimization_barrier((rows, product))
    third = swap(product)
    to_core = kept(rows[1], offsets, parts, jnp.bfloat16)
    keep = kept(rows[0], offsets, parts, jnp.float32)
    from_core = flip(to_core, 1)
    done = total(keep, from_core, [*first, *second], widths[:2], offsets)
    return total(keep, from_core, third, widths[2:], offsets, done)


def project_gathered(attended, out_weight):
    terms = jnp.dot(
        attended,
        lax.all_gather(out_weight, "seq", axis=1, tiled=True),
        preferred_element_type=jnp.float32,
    )
    return lax.psum_scatter(terms.astype(jnp.bfloat16), "head", scatter_dimension=1, tiled=True)


def local(queries, key_rows, value_rows, out_weight):
    kv = jnp.stack([key_rows, value_rows])
    chips = lax.axis_size("seq") // 2
    if chips == 8 and lax.axis_size("head") == 2 and out_weight.shape[1] % 32 == 0:
        return project_on_ring(queries, kv, out_weight)
    attended = attend(queries, exchange_blocks(kv))
    return project_gathered(attended, out_weight)


def solution(mesh):
    in_specs = (P("seq", "head"), P("seq", "head"), P("seq", "head"), P("head", "seq"))
    out_specs = P("seq", "head")
    return jax.shard_map(local, mesh=mesh, in_specs=in_specs, out_specs=out_specs, check_vma=False)
```

```python
import functools
import math

import jax
import jax.numpy as jnp
from jax import lax
from jax.experimental import pallas as pl
from jax.experimental.pallas import tpu as pltpu
from jax.sharding import PartitionSpec as P

HD = 128
BLK = 256

masked_score = -1e30
vmem_limit = 20 * 2**20
in_vmem = pl.BlockSpec(memory_space=pltpu.VMEM)


def call_kernel(body, out_shape, operands, scratch=()):
    many = isinstance(out_shape, (list, tuple))
    return pl.pallas_call(
        body,
        out_shape=out_shape,
        in_specs=[in_vmem] * len(operands),
        out_specs=[in_vmem] * len(out_shape) if many else in_vmem,
        scratch_shapes=list(scratch),
        compiler_params=pltpu.CompilerParams(vmem_limit_bytes=vmem_limit),
        cost_estimate=pl.CostEstimate(flops=1, bytes_accessed=1, transcendentals=0),
    )(*operands)


def flip(value, mask):
    pairs = [(source, source ^ mask) for source in range(lax.axis_size("seq"))]
    return lax.ppermute(value, "seq", pairs)


def attention_body(blocks, heads, *refs):
    query_ref, block_refs, out_ref = refs[0], refs[1 : 1 + blocks], refs[1 + blocks]
    rank = lax.axis_index("seq")
    inside = jnp.logical_and(rank > 0, rank < lax.axis_size("seq") - 1)
    bias = jnp.where(inside, 0.0, masked_score).astype(jnp.float32)
    scale = math.log2(math.e) / math.sqrt(HD)

    def scores_of(head):
        query = query_ref[:, head * HD : (head + 1) * HD]
        scores = [
            lax.dot_general(
                query, ref[0], (((1,), (1,)), ((), ())), preferred_element_type=jnp.float32
            )
            for ref in block_refs
        ]
        scores[-1] = scores[-1] + bias
        return scores

    scores = scores_of(0)
    for head in range(heads):
        later = scores_of(head + 1) if head + 1 < heads else None
        peak = jnp.max(functools.reduce(jnp.maximum, scores), axis=1, keepdims=True) * scale
        weights = [jnp.exp2(part * scale - peak) for part in scores]
        weight_sum = jnp.sum(functools.reduce(jnp.add, weights), axis=1, keepdims=True)
        numerator = functools.reduce(
            jnp.add,
            [
                jnp.dot(part.astype(jnp.bfloat16), ref[1], preferred_element_type=jnp.float32)
                for part, ref in zip(weights, block_refs)
            ],
        )
        out_ref[:, head * HD : (head + 1) * HD] = (numerator / weight_sum).astype(jnp.bfloat16)
        scores = later


def attend(queries, pieces):
    blocks, width = len(pieces), queries.shape[1]
    return call_kernel(
        functools.partial(attention_body, blocks, width // HD),
        jax.ShapeDtypeStruct(queries.shape, jnp.bfloat16),
        [queries, *pieces],
    )


def staged_body(from_ref, to_ref):
    to_ref[...] = from_ref[...]


def staged(value):
    shape = jax.ShapeDtypeStruct(value.shape, value.dtype)
    return call_kernel(staged_body, shape, [value])


def exchange_blocks(rows, early=()):
    count = lax.axis_size("seq")
    bits = count.bit_length() - 1
    outer = [(i, i + 1) for i in range(1, count - 1, 2)]
    outer = outer + [(j, i) for i, j in outer]
    far = [flip(rows, 1 << bit) for bit in range(bits - 1, 1, -1)]
    beside = lax.ppermute(rows, "seq", outer)
    rows = after(rows, early)
    return [rows, flip(rows, 1), flip(rows, 2)] + far + [beside]


def after(value, earlier):
    return lax.optimization_barrier((value, earlier))[0]


class Ring:
    def __init__(self):
        self.count = lax.axis_size("seq")
        self.layers = self.count // 4
        self.chips = self.count // 2

    def place(self, index):
        layer = jnp.where(index < self.layers, index, self.chips - 1 - index)
        return layer, (index >= self.layers).astype(jnp.int32)

    def index(self):
        rank = lax.axis_index("seq")
        layer = rank // 4
        return jnp.where(rank // 2 % 2 == 0, layer, self.chips - 1 - layer)

    def shift(self, value, step):
        def rank_of(index):
            index = index % self.chips
            return 4 * index if index < self.layers else 4 * (self.chips - 1 - index) + 2

        pairs = [
            (rank_of(index) + core, rank_of(index + step) + core)
            for index in range(self.chips)
            for core in (0, 1)
        ]
        return lax.ppermute(value, "seq", pairs)

    def offsets(self):
        steps = [0]
        for step in range(1, self.chips // 2):
            steps += [step, -step]
        return steps + [self.chips // 2]

    def side_and_slot(self, offset):
        layer, across = self.place(lax.rem(self.index() + offset + self.chips, self.chips))
        per_side = self.layers // 2
        return layer // per_side, 2 * lax.rem(layer, per_side) + across

    def ranks(self, side, offsets):
        before, answer = jnp.int32(0), []
        for offset in offsets:
            belongs = self.side_and_slot(offset)[0] == side
            answer.append((belongs, before))
            before = before + belongs.astype(jnp.int32)
        return answer


def hold(held, start, refs):
    for ref in refs:
        held[pl.ds(pl.multiple_of(start, 16), ref.shape[0]), :] = ref[...]
        start = start + ref.shape[0]


def grouped(refs, offsets):
    return [refs[at : at + 1] if at < len(offsets) - 1 else refs[at:] for at in range(len(offsets))]


def times(weight, rows_ref):
    return lax.dot_general(
        weight, rows_ref[...], (((1,), (1,)), ((), ())), preferred_element_type=jnp.float32
    )


def sent_body(first, width, offsets, *refs):
    (mine_ref, theirs_ref), parts = refs[:2], grouped(refs[2:-3], offsets)
    to_same_ref, to_other_ref, held = refs[-3:]
    step = held.shape[0] // width
    ranks = Ring().ranks(1 - lax.axis_index("head"), offsets)
    for (belongs, rank), part in zip(ranks, parts):
        for slot in range(width):

            @pl.when(jnp.logical_and(belongs, rank == first + slot))
            def _():
                hold(held, slot * step, part)

    to_same_ref[...] = times(held[...], mine_ref).astype(jnp.bfloat16)
    to_other_ref[...] = times(held[...], theirs_ref).astype(jnp.bfloat16)


def sent(rows, first, width, offsets, parts):
    step, depth = parts[0].shape
    shape = jax.ShapeDtypeStruct((width * step, rows[0].shape[0]), jnp.bfloat16)
    return call_kernel(
        functools.partial(sent_body, first, width, offsets),
        [shape, shape],
        [*rows, *parts],
        scratch=[pltpu.VMEM((width * step, depth), jnp.bfloat16)],
    )


def last_body(offsets, *refs):
    (mine_ref, theirs_ref, before_ref), parts = refs[:3], grouped(refs[3:-4], offsets)
    to_same_ref, to_other_ref, to_core_ref, held = refs[-4:]
    ring, head = Ring(), lax.axis_index("head")
    rank = len(offsets) // 2 - 1
    for (belongs, before), part in zip(ring.ranks(1 - head, offsets), parts):

        @pl.when(jnp.logical_and(belongs, before == rank))
        def _():
            hold(held, 0, part)

    to_same_ref[...] = times(held[...], mine_ref).astype(jnp.bfloat16)
    to_other_ref[...] = times(held[...], theirs_ref).astype(jnp.bfloat16)
    to_core_ref[...] = before_ref[...]
    side, slot = ring.side_and_slot(offsets[-1])

    @pl.when(side == head)
    def _():
        hold(held, 0, parts[-1])
        there = pl.ds(pl.multiple_of(slot * held.shape[0], 16), held.shape[0])
        to_core_ref[there, :] = times(held[...], theirs_ref).astype(jnp.bfloat16)


def last(rows, before, offsets, parts):
    step, depth = parts[0].shape
    shape = jax.ShapeDtypeStruct((step, rows[0].shape[0]), jnp.bfloat16)
    to_same, to_other, to_core = call_kernel(
        functools.partial(last_body, offsets),
        [shape, shape, jax.ShapeDtypeStruct(before.shape, before.dtype)],
        [*rows, before, *parts],
        scratch=[pltpu.VMEM((step, depth), jnp.bfloat16)],
    )
    return [to_same, to_other], to_core


def kept_body(offsets, *refs):
    rows_ref, parts, (out_ref, held) = refs[0], grouped(refs[1:-2], offsets), refs[-2:]
    ring, head = Ring(), lax.axis_index("head")
    step = held.shape[0] // (ring.chips // 2)
    if len(offsets) < ring.chips:
        held[...] = jnp.zeros(held.shape, held.dtype)
    for offset, part in zip(offsets, parts):
        side, slot = ring.side_and_slot(offset)

        @pl.when(side == head)
        def _():
            hold(held, slot * step, part)

    out_ref[...] = times(held[...], rows_ref).astype(out_ref.dtype)


def kept(rows, offsets, parts, dtype):
    step, depth = parts[0].shape
    shape = (step * (Ring().chips // 2), rows.shape[0])
    return call_kernel(
        functools.partial(kept_body, offsets),
        jax.ShapeDtypeStruct(shape, dtype),
        [rows, *parts],
        scratch=[pltpu.VMEM((shape[0], depth), jnp.bfloat16)],
    )


def total_body(offsets, widths, first, *refs):
    ring = Ring()
    keep_ref, from_core_ref = refs[:2]
    (*received, out_ref, turned) = refs[2:]
    done_ref = received.pop(0) if first else None
    slots = len(offsets) // 2
    step = keep_ref.shape[0] // slots
    core = lax.axis_index("seq") % 2
    ranks = ring.ranks(lax.axis_index("head"), offsets)
    tokens = keep_ref.shape[1]
    row = lax.broadcasted_iota(jnp.int32, (tokens, tokens), 0)
    column = lax.broadcasted_iota(jnp.int32, (tokens, tokens), 1)
    identity = jnp.where(row == column, 1.0, 0.0).astype(jnp.bfloat16)
    if not first:
        turned[...] = jnp.zeros(turned.shape, turned.dtype)
    entry, slot = first, None
    for same_ref, other_ref, width in zip(received[0::2], received[1::2], widths):
        for at in range(width):
            slot = jnp.int32(0)
            for offset, (belongs, rank) in zip(offsets, ranks):
                here = jnp.logical_and(belongs, rank == entry)
                slot = jnp.where(here, ring.side_and_slot(offset)[1], slot)
            entry += 1
            rows = pl.ds(pl.multiple_of(slot * step, 16), step)
            there = slice(at * step, (at + 1) * step)
            for where, kept_ref, ref in (
                (core, keep_ref, same_ref),
                (1 - core, from_core_ref, other_ref),
            ):
                both = kept_ref[rows, :].astype(jnp.float32) + ref[there, :].astype(jnp.float32)
                start = where * step if first else (2 * slot + where) * step
                turned[pl.ds(pl.multiple_of(start, 16), step), :] = both.astype(jnp.bfloat16)
    values = times(identity, turned).astype(jnp.bfloat16)
    if not first:
        out_ref[...] = values
        return
    out_ref[...] = done_ref[...]
    for at in range(slots):

        @pl.when(slot == at)
        def _():
            out_ref[:, 2 * at * step : 2 * (at + 1) * step] = values


def total(keep, from_core, received, widths, offsets, done=None):
    columns, rows = keep.shape
    first = 0 if done is None else len(offsets) // 2 - sum(widths)
    held = 2 * columns if done is None else 4 * columns // len(offsets)
    return call_kernel(
        functools.partial(total_body, offsets, widths, first),
        jax.ShapeDtypeStruct((rows, 2 * columns), jnp.bfloat16),
        [keep, from_core, *([] if done is None else [done]), *received],
        scratch=[pltpu.VMEM((held, rows), jnp.bfloat16)],
    )


def project_on_ring(queries, kv, out_weight):
    ring = Ring()
    shard = out_weight.T
    half = shard.shape[0] // 2
    count = lax.axis_size("seq")
    offsets, widths = ring.offsets(), (1, 2, 1)

    def both_ways(onward, back):
        return [ring.shift(onward, -1), ring.shift(back, 1)]

    def swap(products):
        same, other = products
        crossed = [(2 * i + h, 2 * (i ^ 1) + 1 - h) for i in range(count) for h in range(2)]
        return [
            lax.ppermute(same, "head", [(0, 1), (1, 0)]),
            lax.ppermute(other, ("seq", "head"), crossed),
        ]

    pair = both_ways(shard, shard)
    parts = [shard, *pair]
    queries = staged(queries)
    pieces = exchange_blocks(kv, (queries, pair[0]))
    pair, pieces[1:] = lax.optimization_barrier((pair, pieces[1:]))
    pair = both_ways(*pair)
    parts += pair
    attended = attend(queries, pieces)
    rows = [attended, flip(attended, 1)]
    first = swap(sent(rows, 0, 1, offsets[:5], parts))
    pair = [after(shard, attended) for shard in pair]
    pair = both_ways(*pair)
    parts += pair
    product = sent(rows, 1, 2, offsets[:7], parts)
    pair = [after(shard, (first, product)) for shard in pair]
    second = swap(product)
    before = kept(rows[1], offsets[:7], parts, jnp.bfloat16)
    opposite = both_ways(pair[0][:half], pair[1][half:])
    parts += opposite
    parts[-2:], second = lax.optimization_barrier((parts[-2:], second))
    product, to_core = last(rows, before, offsets, parts)
    rows, product = lax.optimization_barrier((rows, product))
    third = swap(product)
    keep = kept(rows[0], offsets, parts, jnp.float32)
    from_core = flip(to_core, 1)
    done = total(keep, from_core, [*first, *second], widths[:2], offsets)
    return total(keep, from_core, third, widths[2:], offsets, done)


def project_gathered(attended, out_weight):
    terms = jnp.dot(
        attended,
        lax.all_gather(out_weight, "seq", axis=1, tiled=True),
        preferred_element_type=jnp.float32,
    )
    return lax.psum_scatter(terms.astype(jnp.bfloat16), "head", scatter_dimension=1, tiled=True)


def local(queries, key_rows, value_rows, out_weight):
    kv = jnp.stack([key_rows, value_rows])
    chips = lax.axis_size("seq") // 2
    if chips == 8 and lax.axis_size("head") == 2 and out_weight.shape[1] % 32 == 0:
        return project_on_ring(queries, kv, out_weight)
    attended = attend(queries, exchange_blocks(kv))
    return project_gathered(attended, out_weight)


def solution(mesh):
    in_specs = (P("seq", "head"), P("seq", "head"), P("seq", "head"), P("head", "seq"))
    out_specs = P("seq", "head")
    return jax.shard_map(local, mesh=mesh, in_specs=in_specs, out_specs=out_specs, check_vma=False)
```

```python
import functools
import math

import jax
import jax.numpy as jnp
from jax import lax
from jax.experimental import pallas as pl
from jax.experimental.pallas import tpu as pltpu
from jax.sharding import PartitionSpec as P

HD = 128
LANES = 128
BLK = 256

masked_score = -1e30
vmem_limit = 20 * 2**20
in_vmem = pl.BlockSpec(memory_space=pltpu.VMEM)


def call_kernel(body, out_shape, operands, scratch=(), out_spec=in_vmem):
    many = isinstance(out_shape, (list, tuple))
    return pl.pallas_call(
        body,
        out_shape=out_shape,
        in_specs=[in_vmem] * len(operands),
        out_specs=[out_spec] * len(out_shape) if many else out_spec,
        scratch_shapes=list(scratch),
        compiler_params=pltpu.CompilerParams(vmem_limit_bytes=vmem_limit),
        cost_estimate=pl.CostEstimate(flops=1, bytes_accessed=1, transcendentals=0),
    )(*operands)


def flip(value, mask):
    pairs = [(source, source ^ mask) for source in range(lax.axis_size("seq"))]
    return lax.ppermute(value, "seq", pairs)


def attention_body(blocks, heads, *refs):
    query_ref, block_refs, out_ref = refs[0], refs[1 : 1 + blocks], refs[1 + blocks]
    rank = lax.axis_index("seq")
    inside = jnp.logical_and(rank > 0, rank < lax.axis_size("seq") - 1)
    bias = jnp.where(inside, 0.0, masked_score).astype(jnp.float32)
    scale = math.log2(math.e) / math.sqrt(HD)

    def scores_of(head):
        query = query_ref[:, head * HD : (head + 1) * HD]
        scores = [
            lax.dot_general(
                query, ref[0], (((1,), (1,)), ((), ())), preferred_element_type=jnp.float32
            )
            for ref in block_refs
        ]
        scores[-1] = scores[-1] + bias
        return scores

    scores = scores_of(0)
    for head in range(heads):
        later = scores_of(head + 1) if head + 1 < heads else None
        peak = jnp.max(functools.reduce(jnp.maximum, scores), axis=1, keepdims=True) * scale
        weights = [jnp.exp2(part * scale - peak) for part in scores]
        weight_sum = jnp.sum(functools.reduce(jnp.add, weights), axis=1, keepdims=True)
        numerator = functools.reduce(
            jnp.add,
            [
                jnp.dot(part.astype(jnp.bfloat16), ref[1], preferred_element_type=jnp.float32)
                for part, ref in zip(weights, block_refs)
            ],
        )
        out_ref[:, head * HD : (head + 1) * HD] = (numerator / weight_sum).astype(jnp.bfloat16)
        scores = later


def attend(queries, pieces):
    blocks, width = len(pieces), queries.shape[1]
    return call_kernel(
        functools.partial(attention_body, blocks, width // HD),
        jax.ShapeDtypeStruct(queries.shape, jnp.bfloat16),
        [queries, *pieces],
    )


def staged_body(from_ref, to_ref):
    to_ref[...] = from_ref[...]


def staged(value):
    shape = jax.ShapeDtypeStruct(value.shape, value.dtype)
    return call_kernel(staged_body, shape, [value])


def exchange_blocks(rows, early=()):
    count = lax.axis_size("seq")
    bits = count.bit_length() - 1
    outer = [(i, i + 1) for i in range(1, count - 1, 2)]
    outer = outer + [(j, i) for i, j in outer]
    far = [flip(rows, 1 << bit) for bit in range(bits - 1, 1, -1)]
    beside = lax.ppermute(rows, "seq", outer)
    rows = after(rows, early)
    return [rows, flip(rows, 1), flip(rows, 2)] + far + [beside]


def after(value, earlier):
    return lax.optimization_barrier((value, earlier))[0]


class Ring:
    def __init__(self):
        self.count = lax.axis_size("seq")
        self.layers = self.count // 4
        self.chips = self.count // 2

    def place(self, index):
        layer = jnp.where(index < self.layers, index, self.chips - 1 - index)
        return layer, (index >= self.layers).astype(jnp.int32)

    def index(self):
        rank = lax.axis_index("seq")
        layer = rank // 4
        return jnp.where(rank // 2 % 2 == 0, layer, self.chips - 1 - layer)

    def shift(self, value, step):
        def rank_of(index):
            index = index % self.chips
            return 4 * index if index < self.layers else 4 * (self.chips - 1 - index) + 2

        pairs = [
            (rank_of(index) + core, rank_of(index + step) + core)
            for index in range(self.chips)
            for core in (0, 1)
        ]
        return lax.ppermute(value, "seq", pairs)

    def offsets(self):
        steps = [0]
        for step in range(1, self.chips // 2):
            steps += [step, -step]
        return steps + [self.chips // 2]

    def side_and_slot(self, offset):
        layer, across = self.place(lax.rem(self.index() + offset + self.chips, self.chips))
        per_side = self.layers // 2
        return layer // per_side, 2 * lax.rem(layer, per_side) + across

    def ranks(self, side, offsets):
        before, answer = jnp.int32(0), []
        for offset in offsets:
            belongs = self.side_and_slot(offset)[0] == side
            answer.append((belongs, before))
            before = before + belongs.astype(jnp.int32)
        return answer


def hold(held, start, refs):
    for ref in refs:
        held[pl.ds(pl.multiple_of(start, 16), ref.shape[0]), :] = ref[...]
        start = start + ref.shape[0]


def grouped(refs, offsets):
    return [refs[at : at + 1] if at < len(offsets) - 1 else refs[at:] for at in range(len(offsets))]


def times(weight, rows_ref):
    return lax.dot_general(
        weight, rows_ref[...], (((1,), (1,)), ((), ())), preferred_element_type=jnp.float32
    )


def sent_body(first, offsets, fresh, *refs):
    (mine_ref, theirs_ref), (to_same_ref, to_other_ref, held) = refs[:2], refs[-3:]
    before_refs, parts = refs[2 : len(refs) - 3 - len(offsets)], refs[-3 - len(offsets) : -3]
    ranks = Ring().ranks(1 - lax.axis_index("head"), offsets)
    for (belongs, rank), ref in zip(ranks, parts):

        @pl.when(jnp.logical_and(belongs, rank == first))
        def _():
            hold(held, 0, [ref])

    for out_ref, before_ref in zip((to_same_ref, to_other_ref), before_refs):
        out_ref[:fresh, :] = before_ref[...]
    to_same_ref[fresh:, :] = times(held[...], mine_ref).astype(jnp.bfloat16)
    to_other_ref[fresh:, :] = times(held[...], theirs_ref).astype(jnp.bfloat16)


def sent(rows, first, offsets, parts, before=()):
    step, depth = parts[0].shape
    fresh = before[0].shape[0] if before else 0
    shape = jax.ShapeDtypeStruct((fresh + step, rows[0].shape[0]), jnp.bfloat16)
    return call_kernel(
        functools.partial(sent_body, first, offsets, fresh),
        [shape, shape],
        [*rows, *before, *parts],
        scratch=[pltpu.VMEM((step, depth), jnp.bfloat16)],
    )


def last_body(offsets, *refs):
    (mine_ref, theirs_ref, before_ref), parts = refs[:3], grouped(refs[3:-4], offsets)
    to_same_ref, to_other_ref, to_core_ref, held = refs[-4:]
    ring, head = Ring(), lax.axis_index("head")
    rank = len(offsets) // 2 - 1
    for (belongs, before), part in zip(ring.ranks(1 - head, offsets), parts):

        @pl.when(jnp.logical_and(belongs, before == rank))
        def _():
            hold(held, 0, part)

    to_same_ref[...] = times(held[...], mine_ref).astype(jnp.bfloat16)
    to_other_ref[...] = times(held[...], theirs_ref).astype(jnp.bfloat16)
    to_core_ref[...] = before_ref[...]
    side, slot = ring.side_and_slot(offsets[-1])

    @pl.when(side == head)
    def _():
        hold(held, 0, parts[-1])
        there = pl.ds(pl.multiple_of(slot * held.shape[0], 16), held.shape[0])
        to_core_ref[there, :] = times(held[...], theirs_ref).astype(jnp.bfloat16)


def last(rows, before, offsets, parts):
    step, depth = parts[0].shape
    shape = jax.ShapeDtypeStruct((step, rows[0].shape[0]), jnp.bfloat16)
    to_same, to_other, to_core = call_kernel(
        functools.partial(last_body, offsets),
        [shape, shape, jax.ShapeDtypeStruct(before.shape, before.dtype)],
        [*rows, before, *parts],
        scratch=[pltpu.VMEM((step, depth), jnp.bfloat16)],
    )
    return [to_same, to_other], to_core


def kept_body(offsets, *refs):
    rows_ref, parts, (out_ref, held) = refs[0], grouped(refs[1:-2], offsets), refs[-2:]
    ring, head = Ring(), lax.axis_index("head")
    step = held.shape[0] // (ring.chips // 2)
    if len(offsets) < ring.chips:
        held[...] = jnp.zeros(held.shape, held.dtype)
    for offset, part in zip(offsets, parts):
        side, slot = ring.side_and_slot(offset)

        @pl.when(side == head)
        def _():
            hold(held, slot * step, part)

    out_ref[...] = times(held[...], rows_ref).astype(out_ref.dtype)


def kept(rows, offsets, parts, dtype):
    step, depth = parts[0].shape
    shape = (step * (Ring().chips // 2), rows.shape[0])
    return call_kernel(
        functools.partial(kept_body, offsets),
        jax.ShapeDtypeStruct(shape, dtype),
        [rows, *parts],
        scratch=[pltpu.VMEM((shape[0], depth), jnp.bfloat16)],
    )


def summed(offsets, entries, keep_ref, from_core_ref, received, turned, alone):
    ring = Ring()
    step = 2 * keep_ref.shape[0] // len(offsets)
    core = lax.axis_index("seq") % 2
    ranks = ring.ranks(lax.axis_index("head"), offsets)
    slot = jnp.int32(0)
    for entry, same_ref, other_ref, at in zip(entries, *received):
        slot = jnp.int32(0)
        for offset, (belongs, rank) in zip(offsets, ranks):
            here = jnp.logical_and(belongs, rank == entry)
            slot = jnp.where(here, ring.side_and_slot(offset)[1], slot)
        rows = pl.ds(pl.multiple_of(slot * step, 16), step)
        there = slice(at * step, (at + 1) * step)
        for where, kept_ref, ref in (
            (core, keep_ref, same_ref),
            (1 - core, from_core_ref, other_ref),
        ):
            both = kept_ref[rows, :].astype(jnp.float32) + ref[there, :].astype(jnp.float32)
            start = where * step if alone else (2 * slot + where) * step
            turned[pl.ds(pl.multiple_of(start, 16), step), :] = both.astype(jnp.bfloat16)
    return slot


def by_tokens(turned):
    tokens = turned.shape[1]
    row = lax.broadcasted_iota(jnp.int32, (tokens, tokens), 0)
    column = lax.broadcasted_iota(jnp.int32, (tokens, tokens), 1)
    identity = jnp.where(row == column, 1.0, 0.0).astype(jnp.bfloat16)
    return times(identity, turned).astype(jnp.bfloat16)


def total_body(offsets, widths, keep_ref, from_core_ref, *refs):
    (*received, out_ref, turned) = refs
    turned[...] = jnp.zeros(turned.shape, turned.dtype)
    pairs = [
        (same_ref, other_ref, at)
        for same_ref, other_ref, width in zip(received[0::2], received[1::2], widths)
        for at in range(width)
    ]
    entries = range(len(pairs))
    summed(offsets, entries, keep_ref, from_core_ref, list(zip(*pairs)), turned, False)
    out_ref[...] = by_tokens(turned)


def total(keep, from_core, received, widths, offsets):
    columns, rows = keep.shape
    return call_kernel(
        functools.partial(total_body, offsets, widths),
        jax.ShapeDtypeStruct((rows, 2 * columns), jnp.bfloat16),
        [keep, from_core, *received],
        scratch=[pltpu.VMEM((2 * columns, rows), jnp.bfloat16)],
    )


def windows(slots, width):
    answer = []
    for slot in range(slots):
        low, high = slot * width, (slot + 1) * width
        answer.append((low, high, low // LANES * LANES, -(-high // LANES) * LANES))
    return answer


def finish_body(offsets, keep_ref, from_core_ref, done_ref, same_ref, other_ref, out_ref, turned, window, sems):
    slots = len(offsets) // 2
    places = windows(slots, turned.shape[0])
    ring, head = Ring(), lax.axis_index("head")
    slot = jnp.int32(0)
    for offset, (belongs, rank) in zip(offsets, ring.ranks(head, offsets)):
        here = jnp.logical_and(belongs, rank == slots - 1)
        slot = jnp.where(here, ring.side_and_slot(offset)[1], slot)

    def copies(left, right):
        sides = [(0, left), (right, out_ref.shape[1])]
        return [
            pltpu.make_async_copy(done_ref.at[:, low:high], out_ref.at[:, low:high], sems.at[at])
            for at, (low, high) in enumerate(sides)
            if high > low
        ]

    for at, (_, _, left, right) in enumerate(places):

        @pl.when(slot == at)
        def _():
            for copy in copies(left, right):
                copy.start()

    received = [[same_ref], [other_ref], [0]]
    summed(offsets, [slots - 1], keep_ref, from_core_ref, received, turned, True)
    values = by_tokens(turned)
    for at, (low, high, left, right) in enumerate(places):

        @pl.when(slot == at)
        def _():
            held = window.at[:, : right - left]
            held[...] = done_ref[:, left:right]
            window[:, low - left : high - left] = values
            last_copy = pltpu.make_async_copy(held, out_ref.at[:, left:right], sems.at[2])
            last_copy.start()
            for copy in copies(left, right):
                copy.wait()
            last_copy.wait()


def finish(keep, from_core, done, received, offsets):
    columns, rows = keep.shape
    slots = len(offsets) // 2
    width = 2 * columns // slots
    widest = max(right - left for _, _, left, right in windows(slots, width))
    return call_kernel(
        functools.partial(finish_body, offsets),
        jax.ShapeDtypeStruct((rows, 2 * columns), jnp.bfloat16),
        [keep, from_core, done, *received],
        scratch=[
            pltpu.VMEM((width, rows), jnp.bfloat16),
            pltpu.VMEM((rows, widest), jnp.bfloat16),
            pltpu.SemaphoreType.DMA((3,)),
        ],
        out_spec=pl.BlockSpec(memory_space=pl.ANY),
    )


def project_on_ring(queries, kv, out_weight):
    ring = Ring()
    shard = out_weight.T
    half = shard.shape[0] // 2
    count = lax.axis_size("seq")
    offsets, widths = ring.offsets(), (1, 2, 1)

    def both_ways(onward, back):
        return [ring.shift(onward, -1), ring.shift(back, 1)]

    def swap(products):
        same, other = products
        crossed = [(2 * i + h, 2 * (i ^ 1) + 1 - h) for i in range(count) for h in range(2)]
        return [
            lax.ppermute(same, "head", [(0, 1), (1, 0)]),
            lax.ppermute(other, ("seq", "head"), crossed),
        ]

    pair = both_ways(shard, shard)
    parts = [shard, *pair]
    queries = staged(queries)
    pieces = exchange_blocks(kv, (queries, pair[0]))
    pair, pieces[1:] = lax.optimization_barrier((pair, pieces[1:]))
    pair = both_ways(*pair)
    parts += pair
    attended = attend(queries, pieces)
    rows = [attended, flip(attended, 1)]
    first = swap(sent(rows, 0, offsets[:5], parts))
    pair = [after(shard, attended) for shard in pair]
    pair = both_ways(*pair)
    parts += pair
    product = sent(rows, 1, offsets[:6], parts[:6])
    product = sent(rows, 2, offsets[:7], parts, product)
    pair = [after(shard, (first, product)) for shard in pair]
    second = swap(product)
    before = kept(rows[1], offsets[:7], parts, jnp.bfloat16)
    opposite = both_ways(pair[0][:half], pair[1][half:])
    parts += opposite
    parts[-2:], second = lax.optimization_barrier((parts[-2:], second))
    product, to_core = last(rows, before, offsets, parts)
    rows, product = lax.optimization_barrier((rows, product))
    third = swap(product)
    keep = kept(rows[0], offsets, parts, jnp.float32)
    step = shard.shape[0]
    pieces = [to_core[at : at + step] for at in range(0, to_core.shape[0], step)]
    from_core = jnp.concatenate([flip(piece, 1) for piece in pieces], axis=0)
    done = total(keep, from_core, [*first, *second], widths[:2], offsets)
    return finish(keep, from_core, done, third, offsets)


def project_gathered(attended, out_weight):
    terms = jnp.dot(
        attended,
        lax.all_gather(out_weight, "seq", axis=1, tiled=True),
        preferred_element_type=jnp.float32,
    )
    return lax.psum_scatter(terms.astype(jnp.bfloat16), "head", scatter_dimension=1, tiled=True)


def local(queries, key_rows, value_rows, out_weight):
    kv = jnp.stack([key_rows, value_rows])
    chips = lax.axis_size("seq") // 2
    if chips == 8 and lax.axis_size("head") == 2 and out_weight.shape[1] % 32 == 0:
        return project_on_ring(queries, kv, out_weight)
    attended = attend(queries, exchange_blocks(kv))
    return project_gathered(attended, out_weight)


def solution(mesh):
    in_specs = (P("seq", "head"), P("seq", "head"), P("seq", "head"), P("head", "seq"))
    out_specs = P("seq", "head")
    return jax.shard_map(local, mesh=mesh, in_specs=in_specs, out_specs=out_specs, check_vma=False)
```
